128 devices in a mesh: scene: 8 (over y, z_lo), frame: 16 (over x, z_hi, core).
Axes of the slice: x: 4, y: 4, z: 4 (z_hi: 2, z_lo: 2; z = z_hi * 2 + z_lo), core: 2. Of those that a mesh axis runs over, the one named last changes fastest.
Arguments:
- tokens: bfloat16 [16384, 1024], P(('scene', 'frame')), may hold values from -8 to 8
- covisible: int32 [8, 16, 16], P('scene'), may hold values 0 or 1
- w_query: bfloat16 [1024, 1024], replicated, may hold values from -0.1875 to 0.1875
- w_key: bfloat16 [1024, 1024], replicated, may hold values from -0.20625 to 0.20625
- w_value: bfloat16 [1024, 1024], replicated, may hold values from -0.1875 to 0.1875
- w_out: bfloat16 [1024, 1024], replicated, may hold values from -3 to 3
- cotangent: bfloat16 [16384, 1024], P(('scene', 'frame')), may hold values from -24 to 24
Outputs:
- result: bfloat16 [16384, 1024], P(('scene', 'frame'))
- grad_tokens: float32 [16384, 1024], P(('scene', 'frame'))
- grad_out_weight: float32 [1024, 1024], P('frame', 'scene')
The draws below stay inside these ranges and needn't reach their ends.
All inputs are finite; a program needn't handle non-finite values. No bound on the sum of `covisible` on one device may be relied on, other than what follows from the above.
Results may differ from the reference program's by a relative error of at most 0.023.
Values may be sent and summed in bfloat16 or wider, within the bound.
No kernel may reach another device: no remote copies, remote signals or barrier semaphores. Data moves between devices by JAX's collectives and lax.ppermute only.
A program may use at most 128 MiB of HBM per device.

```python
import jax
import jax.numpy as jnp
from jax import lax

D = 1024
HEADS = 16
HEAD_DIM = 64
TOKF = 128
FRAMES_SC = 16
SCENES = 8
TOKENS = 16384
N_SCENE = 8
N_FRAME = 16


def shared_matrix(key):
    base = jax.random.normal(key, (D, D), jnp.float32)
    return jnp.clip(base, -6.0, 6.0) / D ** 0.5


def draw_w_query(key, part):
    base = shared_matrix(key)
    return base.astype(jnp.bfloat16)


def draw_w_key(key, part):
    key = jax.random.fold_in(key, 12)
    own_part = jnp.clip(jax.random.normal(key, (D, D), jnp.float32), -6.0, 6.0) / D ** 0.5
    matrix = own_part
    return matrix.astype(jnp.bfloat16)


def draw_tokens(key, part):
    key = jax.random.fold_in(key, 13)
    normal_key = jax.random.fold_in(key, 0)
    values = jnp.clip(jax.random.normal(normal_key, (TOKENS, D), jnp.float32), -4.0, 4.0)
    return values.astype(jnp.bfloat16)


def with_ends(entries, rng, low, largest):
    extent = entries.shape
    index_at = [jax.random.randint(jax.random.fold_in(rng, axis), (), 0, extent[axis]) for axis in range(len(extent))]
    entries = entries.at[tuple(index_at)].set(low)
    longest = extent.index(max(extent))
    index_at[longest] = (index_at[longest] + 1) % extent[longest]
    return entries.at[tuple(index_at)].set(largest)


def raised(values, key, source, target, blocks, factor):
    owner, partner = [(jnp.arange(values.shape[axis_at]) // (values.shape[axis_at] // blocks)).reshape([-1 if axis == axis_at else 1 for axis in range(values.ndim)]) for axis_at in (source, target)]
    chosen = jax.random.permutation(key, blocks)[partner]
    strong = (owner == chosen) | (owner == (partner + blocks // 2) % blocks)
    return jnp.where(strong, factor * values, values)


def block_levels(key, dims, cuts, least, largest):
    loudness = 1.0
    for dim, blocks in cuts:
        draws = jax.random.uniform(jax.random.fold_in(jax.random.fold_in(key, 6), dim), (blocks,), jnp.float32, least / len(cuts), largest / len(cuts))
        loudness = loudness * jnp.repeat(jnp.exp(draws), dims[dim] // blocks).reshape((-1,) + (1,) * (len(dims) - 1 - dim))
    return loudness


def centred(stream_key, shape, scale, limit, shards=(), dtype=jnp.bfloat16):
    entries = jax.random.normal(stream_key, shape, jnp.float32) * scale
    if len(shards) > 0:
        entries = block_levels(stream_key, shape, shards, -0.22, 0.18) * entries
    return jnp.clip(entries, min=-limit, max=limit).astype(dtype)


def gaussian_with(own_key, dims, deviation, reach, cuts, heavy, held_as=jnp.bfloat16):
    entries = deviation * jax.random.normal(own_key, dims, jnp.float32)
    if cuts:
        entries = entries * block_levels(own_key, dims, cuts, -0.22, 0.18)
    return jnp.clip(raised(entries, jax.random.fold_in(own_key, 3), *heavy), -reach, reach).astype(held_as)


def setup_inputs(seed: int = 0) -> dict:
    key_of = jax.random.split(jax.random.key(seed), 8)
    return {
        "tokens": draw_tokens(jax.random.fold_in(key_of[7], 71), 0),
        "covisible": with_ends((jax.random.randint(key_of[1], (SCENES, FRAMES_SC, FRAMES_SC), 0, 2) < 1).astype(jnp.int32), jax.random.fold_in(key_of[1], 1), 0, 1),
        "w_query": draw_w_query(jax.random.fold_in(key_of[7], 71), 0),
        "w_key": draw_w_key(jax.random.fold_in(key_of[7], 71), 0),
        "w_value": centred(key_of[4], (D, D), D ** -0.5, 0.1875),
        "w_out": centred(key_of[5], (D, D), (16 / D ** 0.5), 3.0),
        "cotangent": gaussian_with(key_of[6], (TOKENS, D), 1.0, 24.0, ((0, 128),), (0, 1, 128, 5.5)),
    }


def scene_block(scene_tokens, scene_pairs, scene_cotangent, w_query, w_key, w_value, w_out):
    row_count = scene_tokens.shape[0]
    frame_ids = (jnp.arange(row_count) // TOKF).astype(jnp.int32)
    same_frame = jnp.arange(N_FRAME)[:, None] == jnp.arange(N_FRAME)[None, :]
    frame_seen = (scene_pairs == 1) | same_frame
    visible = frame_seen[frame_ids[:, None], frame_ids[None, :]]
    score_scale = HEAD_DIM ** -0.5
    query = jnp.dot(scene_tokens, w_query, preferred_element_type=jnp.float32).astype(jnp.bfloat16)
    keys = jnp.dot(scene_tokens, w_key, preferred_element_type=jnp.float32).astype(jnp.bfloat16)
    values = jnp.dot(scene_tokens, w_value, preferred_element_type=jnp.float32).astype(jnp.bfloat16)

    def split_heads(matrix):
        return matrix.reshape(row_count, HEADS, HEAD_DIM).transpose(1, 0, 2)

    def merge_heads(stacked):
        return stacked.transpose(1, 0, 2).reshape(row_count, HEADS * HEAD_DIM)

    def chances_for(query_head, key_head):
        logits = jnp.dot(query_head, key_head.T, preferred_element_type=jnp.float32) * score_scale
        logits = jnp.where(visible, logits, -1e30)
        shifted = jnp.exp(logits - jnp.max(logits, axis=1, keepdims=True))
        return (shifted / jnp.sum(shifted, axis=1, keepdims=True)).astype(jnp.bfloat16)

    def forward_head(operands):
        query_head, key_head, value_head = operands
        return jnp.dot(chances_for(query_head, key_head), value_head, preferred_element_type=jnp.float32)

    query_heads = split_heads(query)
    key_heads = split_heads(keys)
    value_heads = split_heads(values)
    attended_full = lax.map(forward_head, (query_heads, key_heads, value_heads))
    attended = merge_heads(attended_full).astype(jnp.bfloat16)
    result = jnp.dot(attended, w_out, preferred_element_type=jnp.float32).astype(jnp.bfloat16)
    grad_attended = jnp.dot(scene_cotangent, w_out.T, preferred_element_type=jnp.float32).astype(jnp.bfloat16)

    def backward_head(operands):
        query_head, key_head, value_head, grad_head, full_head = operands
        chances = chances_for(query_head, key_head)
        grad_chances = jnp.dot(grad_head, value_head.T, preferred_element_type=jnp.float32)
        row_delta = jnp.sum(grad_head.astype(jnp.float32) * full_head, axis=1, keepdims=True)
        grad_logits = (chances.astype(jnp.float32) * (grad_chances - row_delta) * score_scale).astype(jnp.bfloat16)
        grad_query_head = jnp.dot(grad_logits, key_head, preferred_element_type=jnp.float32)
        grad_key_head = jnp.dot(grad_logits.T, query_head, preferred_element_type=jnp.float32)
        grad_value_head = jnp.dot(chances.T, grad_head, preferred_element_type=jnp.float32)
        return grad_query_head, grad_key_head, grad_value_head

    grad_parts = lax.map(backward_head, (query_heads, key_heads, value_heads, split_heads(grad_attended), attended_full))
    grad_query = merge_heads(grad_parts[0]).astype(jnp.bfloat16)
    grad_key = merge_heads(grad_parts[1]).astype(jnp.bfloat16)
    grad_value = merge_heads(grad_parts[2]).astype(jnp.bfloat16)
    grad_tokens = jnp.dot(grad_query, w_query.T, preferred_element_type=jnp.float32)
    grad_tokens = grad_tokens + jnp.dot(grad_key, w_key.T, preferred_element_type=jnp.float32)
    grad_tokens = grad_tokens + jnp.dot(grad_value, w_value.T, preferred_element_type=jnp.float32)
    out_term = jnp.dot(attended.T, scene_cotangent, preferred_element_type=jnp.float32)
    return result, grad_tokens, out_term


def reference(tokens, covisible, w_query, w_key, w_value, w_out, cotangent):
    scene_rows = N_FRAME * TOKF

    def one_scene(operands):
        scene_tokens, scene_pairs, scene_cotangent = operands
        return scene_block(scene_tokens, scene_pairs, scene_cotangent, w_query, w_key, w_value, w_out)

    outputs = lax.map(one_scene, (tokens.reshape(N_SCENE, scene_rows, D), covisible,
                                  cotangent.reshape(N_SCENE, scene_rows, D)))
    result = outputs[0].reshape(TOKENS, D)
    grad_tokens = outputs[1].reshape(TOKENS, D)
    grad_out_weight = jnp.sum(outputs[2], axis=0)
    return (result, grad_tokens, grad_out_weight)
```

```python
import functools
import math

import jax
import jax.numpy as jnp
from jax import lax
from jax.experimental import pallas as pl
from jax.experimental.pallas import tpu as pltpu
from jax.sharding import PartitionSpec as P

HEAD_DIM = 64
BF = jnp.bfloat16
F32 = jnp.float32
HIDDEN = -1e30
NT = (((1,), (1,)), ((), ()))
VMEM = pl.BlockSpec(memory_space=pltpu.VMEM)
SMEM = pl.BlockSpec(memory_space=pltpu.SMEM)
ANY = pl.BlockSpec(memory_space=pl.ANY)
LOG2E = 1.0 / math.log(2.0)
SCALE = HEAD_DIM**-0.5


def dot(a, b):
    return jnp.dot(a, b, preferred_element_type=F32)


def dot_nt(a, b):
    return lax.dot_general(a, b, NT, preferred_element_type=F32)


def params(limit):
    return dict(
        compiler_params=pltpu.CompilerParams(vmem_limit_bytes=limit * 2**20),
        cost_estimate=pl.CostEstimate(flops=1, bytes_accessed=1, transcendentals=0),
    )


def start_all(pairs, arrived):
    copies = [pltpu.make_async_copy(src, dst, arrived.at[i]) for i, (src, dst) in enumerate(pairs)]
    for copy in copies:
        copy.start()
    return copies


def aligned(index, size):
    return pl.ds(pl.multiple_of(index * size, size), size)


def in_core_order(place, rows_ref, start, own, peer):
    rows = own.shape[0]
    core = place[2]
    rows_ref[pl.ds(pl.multiple_of(start + core * rows, rows), rows), :] = own[...]
    rows_ref[pl.ds(pl.multiple_of(start + (1 - core) * rows, rows), rows), :] = peer[...]


def fetch_kernel(place, wk, wv, wq, wo, columns, rows, pairs, arrived):
    z, core, block = place[1], place[2], place[3]
    chips = pairs.shape[1]
    wide = 2 * HEAD_DIM
    moves = [
        (w.at[:, pl.ds(pl.multiple_of(a * 2 * wide + z * wide, wide), wide)], pairs.at[slot, a])
        for slot, w in enumerate((wk, wv, wq))
        for a in range(chips)
    ]
    for a in range(chips):
        from_rows = aligned(chips * a + block, HEAD_DIM)
        moves.append((wo.at[from_rows, :], rows.at[a * HEAD_DIM : (a + 1) * HEAD_DIM, :]))
    copies = start_all(moves, arrived)

    def keep(slot, lanes):
        for a in range(0, chips, 2):
            both = jnp.concatenate([pairs[slot, a, :, lanes], pairs[slot, a + 1, :, lanes]], axis=1)
            columns[slot, :, a * HEAD_DIM : (a + 2) * HEAD_DIM] = both

    for slot in range(3):
        for a in range(chips):
            copies[slot * chips + a].wait()
        pl.when(core == 0)(functools.partial(keep, slot, slice(0, HEAD_DIM)))
        pl.when(core == 1)(functools.partial(keep, slot, slice(HEAD_DIM, wide)))
    for copy in copies[3 * chips :]:
        copy.wait()


def fetch(place, weights, chips):
    width = weights[0].shape[0]
    block = chips * HEAD_DIM
    return pl.pallas_call(
        fetch_kernel,
        in_specs=[SMEM] + [ANY] * 4,
        out_specs=[VMEM] * 2,
        out_shape=[jax.ShapeDtypeStruct((3, width, block), BF), jax.ShapeDtypeStruct((block, width), BF)],
        scratch_shapes=[
            pltpu.VMEM((3, chips, width, 2 * HEAD_DIM), BF),
            pltpu.SemaphoreType.DMA((4 * chips,)),
        ],
        name="fetch",
        **params(48),
    )(place, *weights)


def project_kernel(place, own, peer, cot, peer_cot, held, held_out, *rest):
    outs, (tok, grads, turned) = rest[:-3], rest[-3:]
    in_core_order(place, tok, 0, own, peer)
    in_core_order(place, grads, 0, cot, peer_cot)
    for slot in range(3):
        part = dot(tok[...], held[slot])
        if slot == 2:
            part = part * (SCALE * LOG2E)
        turned[slot] = part.astype(BF).T
    turned[3] = dot_nt(held_out[...], grads[...]).astype(BF)
    for d, out in enumerate(outs):
        head = lax.rem(place[0] + d, len(outs))
        for slot in range(4):
            out[slot * HEAD_DIM : (slot + 1) * HEAD_DIM, :] = turned[slot, aligned(head, HEAD_DIM), :]


def project(place, tokens, cotangents, weights, chips):
    rows, width = tokens[0].shape
    block = chips * HEAD_DIM
    return pl.pallas_call(
        project_kernel,
        in_specs=[SMEM] + [VMEM] * 6,
        out_specs=[VMEM] * chips,
        out_shape=[jax.ShapeDtypeStruct((4 * HEAD_DIM, 2 * rows), BF)] * chips,
        scratch_shapes=[
            pltpu.VMEM((2 * rows, width), BF),
            pltpu.VMEM((2 * rows, width), BF),
            pltpu.VMEM((4, block, 2 * rows), BF),
        ],
        name="project",
        **params(16),
    )(place, *tokens, *cotangents, *weights)


def frame_at(place, chips, slot, core):
    plane, d = slot // chips, slot % chips
    x = lax.rem(place[0] + chips - d, chips)
    z = lax.rem(place[1] + plane, 2)
    return x * 4 + z * 2 + core


def attend_kernel(chips, step, chunk, place, cov, *rest):
    slots = 2 * chips
    parts, outs, rest = rest[:slots], rest[slots : slots + chips], rest[slots + chips :]
    packed, keys, even, odd, raw_even, raw_odd, att, grad_query, total = rest
    rows = slots * step
    frame_rows = step // 2
    frames = 2 * slots
    lane = lax.broadcasted_iota(jnp.int32, (step, 128), 1)
    half = lax.broadcasted_iota(jnp.int32, (step, 128), 0) // frame_rows
    ones = (lane >= frames) & (lane < frames + 3)
    for slot, part in enumerate(parts):
        at = slot * step
        packed[:, at : at + step] = part[...]
        keys[at : at + step, 0:128] = part[0:128, :].T
        keys[at : at + step, 128:256] = jnp.where((lane == half + 2 * slot) | ones, 1.0, 0.0).astype(BF)
    total[...] = jnp.zeros_like(total)
    chunks = range(0, rows, chunk)
    bias_row = lax.broadcasted_iota(jnp.int32, (frames, frame_rows), 0)
    delta_row = lax.broadcasted_iota(jnp.int32, (16, step), 0)
    rest_rows = jnp.zeros((128 - frames, step), BF)
    last_rows = jnp.zeros((112 - frames, step), BF)
    frame_zeros = jnp.zeros((frames, step), BF)
    sum_rows = jnp.ones((16, chunk), BF)
    zero = jnp.zeros((HEAD_DIM, step), F32)
    none = jnp.zeros((HEAD_DIM, step), BF)

    def columns(ref, first, i):
        return ref[first : first + HEAD_DIM, pl.ds(pl.multiple_of(i * step, step), step)]

    def score_side(i):
        biases = []
        for core in range(2):
            query_frame = frame_at(place, chips, i, core)
            bias = jnp.zeros((frames, frame_rows), F32)
            for key in range(frames):
                key_frame = frame_at(place, chips, key // 2, key % 2)
                seen = jnp.logical_or(cov[0, query_frame, key_frame] == 1, query_frame == key_frame)
                bias = jnp.where(bias_row == key, jnp.where(seen, 0.0, HIDDEN), bias)
            biases.append(bias)
        bias = jnp.concatenate(biases, axis=1).astype(BF)
        return jnp.concatenate([columns(packed, 128, i), none, bias, rest_rows], axis=0)

    def grad_sides(i, inverse, delta):
        grad = columns(packed, 192, i)
        high = delta.astype(BF).astype(F32)
        middle = (delta - high).astype(BF).astype(F32)
        low = delta - high - middle
        deltas = jnp.where(
            delta_row == 0, -high, jnp.where(delta_row == 1, -middle, jnp.where(delta_row == 2, -low, 0.0))
        ).astype(BF)
        query = columns(packed, 128, i).astype(F32) * (inverse * (1.0 / LOG2E))
        back = jnp.concatenate(
            [
                jnp.concatenate([zero, grad.astype(F32) * inverse], axis=0).astype(BF).T,
                jnp.concatenate([query, zero], axis=0).astype(BF).T,
            ],
            axis=0,
        )
        return jnp.concatenate([none, grad, frame_zeros, deltas, last_rows], axis=0), back

    def together(score=None, weigh=None, grad=None):
        if score:
            at_score, logits_to = score
            score_right = score_side(at_score)
            top = jnp.full((8, step), HIDDEN, F32)
        if weigh:
            at_weigh, logits_from, weigh_top, raw_to = weigh
            summed = jnp.zeros((HEAD_DIM + 16, step), F32)
        if grad:
            at_grad, raw_from, inverse, delta = grad
            grad_right, back = grad_sides(at_grad, inverse, delta)
            query_sum = zero
        for c in chunks:
            here = slice(c, c + chunk)
            if score:
                part = dot(keys[here, :], score_right)
                logits_to[here, :] = part
                top = jnp.maximum(top, jnp.max(part.reshape(chunk // 8, 8, step), axis=0))
            if weigh:
                raw = jnp.exp2(logits_from[here, :] - weigh_top).astype(BF)
                raw_to[here, :] = raw
                summed = summed + dot(jnp.concatenate([packed[HEAD_DIM:128, here], sum_rows], axis=0), raw)
            if grad:
                raw = raw_from[here, :]
                change = raw * dot(keys[here, :], grad_right).astype(BF)
                query_sum = query_sum + dot(packed[0:HEAD_DIM, here], change)
                total[here, :] += dot(jnp.concatenate([raw, change], axis=1), back)
        if grad:
            at = pl.ds(pl.multiple_of(at_grad * step, step), step)
            grad_query[:, at] = (query_sum * (inverse * SCALE)).astype(BF)
        got = ()
        if score:
            got += (jnp.max(top, axis=0, keepdims=True),)
        if weigh:
            inverse = 1.0 / summed[HEAD_DIM : HEAD_DIM + 1, :]
            attended = summed[0:HEAD_DIM, :] * inverse
            att[:, pl.ds(pl.multiple_of(at_weigh * step, step), step)] = attended.astype(BF)
            delta = jnp.sum(columns(packed, 192, at_weigh).astype(F32) * attended, axis=0, keepdims=True)
            got += (inverse, delta)
        return got

    (top,) = together(score=(0, even))
    carry = together(score=(1, odd), weigh=(0, even, top, raw_even))

    def body(j, carry):
        i = 2 * j + 1
        top, inverse, delta = carry
        top, inverse, delta = together((i + 1, even), (i, odd, top, raw_odd), (i - 1, raw_even, inverse, delta))
        return together((i + 2, odd), (i + 1, even, top, raw_even), (i, raw_odd, inverse, delta))

    top, inverse, delta = lax.fori_loop(0, slots // 2 - 1, body, carry)
    inverse, delta = together(
        weigh=(slots - 1, odd, top, raw_odd), grad=(slots - 2, raw_even, inverse, delta)
    )
    together(grad=(slots - 1, raw_odd, inverse, delta))
    for slot in range(slots):
        here = slice(slot * step, (slot + 1) * step)
        there = slice(slot // chips * step, (slot // chips + 1) * step)
        out = outs[slot % chips]
        out[0:HEAD_DIM, there] = grad_query[:, here]
        out[HEAD_DIM : 3 * HEAD_DIM, there] = total[here, :].astype(BF).T
        out[3 * HEAD_DIM : 4 * HEAD_DIM, there] = att[:, here]


def attend(place, pairs, parts, chips):
    step = parts[0].shape[1]
    slots = 2 * chips
    rows = slots * step
    return pl.pallas_call(
        functools.partial(attend_kernel, chips, step, 1024),
        in_specs=[SMEM, SMEM] + [VMEM] * slots,
        out_specs=[VMEM] * chips,
        out_shape=[jax.ShapeDtypeStruct((4 * HEAD_DIM, 2 * step), BF)] * chips,
        scratch_shapes=[
            pltpu.VMEM((4 * HEAD_DIM, rows), BF),
            pltpu.VMEM((rows, 256), BF),
            pltpu.VMEM((rows, step), F32),
            pltpu.VMEM((rows, step), F32),
            pltpu.VMEM((rows, step), BF),
            pltpu.VMEM((rows, step), BF),
            pltpu.VMEM((HEAD_DIM, rows), BF),
            pltpu.VMEM((HEAD_DIM, rows), BF),
            pltpu.VMEM((rows, 128), F32),
        ],
        name="attend",
        **params(40),
    )(place, pairs, *parts)


def finish_kernel(place, held, held_out, *rest):
    parts, (near, far, send, turned, wide) = rest[:-5], rest[-5:]
    chips = len(parts)
    rows, width = near.shape[0], held.shape[1]
    core = place[2]
    for d, part in enumerate(parts):
        head = lax.rem(place[0] + d, chips)
        for slot in range(4):
            turned[slot, aligned(head, HEAD_DIM), :] = part[slot * HEAD_DIM : (slot + 1) * HEAD_DIM, :]
    terms = None
    for slot, weight in enumerate((2, 0, 1)):
        term = dot_nt(turned[slot].T, held[weight])
        terms = term if terms is None else terms + term
    wide[:, 0:width] = terms
    wide[:, width : 2 * width] = dot(turned[3].T, held_out[...])
    near[...] = wide[aligned(core, rows), :]
    far[...] = wide[aligned(2 + core, rows), :]
    send[0:rows, :] = wide[aligned(1 - core, rows), :].astype(BF)
    send[rows : 2 * rows, :] = wide[aligned(3 - core, rows), :].astype(BF)


def finish(place, parts, weights):
    chips = len(parts)
    rows, width = parts[0].shape[1] // 4, weights[0].shape[1]
    block = chips * HEAD_DIM
    keep = jax.ShapeDtypeStruct((rows, 2 * width), F32)
    return pl.pallas_call(
        finish_kernel,
        in_specs=[SMEM] + [VMEM] * (2 + chips),
        out_specs=[VMEM] * 3,
        out_shape=[keep, keep, jax.ShapeDtypeStruct((2 * rows, 2 * width), BF)],
        scratch_shapes=[pltpu.VMEM((4, block, 4 * rows), BF), pltpu.VMEM((4 * rows, 2 * width), F32)],
        name="finish",
        **params(24),
    )(place, *weights, *parts)


def out_terms_kernel(place, *rest):
    parts, cots, rest = rest[0:4], rest[4:8], rest[8:]
    outs, (turned, cot, wide) = rest[:-3], rest[-3:]
    rows = cots[0].shape[0]
    in_core_order(place, cot, 0, cots[0], cots[1])
    in_core_order(place, cot, 2 * rows, cots[2], cots[3])
    for d, part in enumerate(parts):
        turned[aligned(lax.rem(place[0] + d, len(parts)), HEAD_DIM), :] = part[3 * HEAD_DIM : 4 * HEAD_DIM, :]
    wide[...] = dot(turned[...], cot[...])
    for d, out in enumerate(outs):
        out[...] = wide[:, aligned(lax.rem(place[4] + d, len(outs)), out.shape[1])].astype(BF)


def out_terms(place, parts, cotangents, cuts):
    chips = len(parts)
    rows, width = cotangents[0].shape
    block = chips * HEAD_DIM
    return pl.pallas_call(
        out_terms_kernel,
        in_specs=[SMEM] + [VMEM] * (chips + 4),
        out_specs=[VMEM] * cuts,
        out_shape=[jax.ShapeDtypeStruct((block, width // cuts), BF)] * cuts,
        scratch_shapes=[
            pltpu.VMEM((block, 4 * rows), BF),
            pltpu.VMEM((4 * rows, width), BF),
            pltpu.VMEM((block, width), F32),
        ],
        name="out_terms",
        **params(16),
    )(place, *parts, *cotangents)


def added(parts):
    total = parts[0][...].astype(F32)
    for part in parts[1:]:
        total = total + part[...].astype(F32)
    return total


def sum_heads_kernel(chips, place, *rest):
    parts, outs, wide = rest[: -1 - chips], rest[-1 - chips : -1], rest[-1]
    wide[...] = added(parts)
    for d, out in enumerate(outs):
        out[...] = wide[aligned(lax.rem(place[0] + d, chips), HEAD_DIM), :].astype(out.dtype)


def sum_heads(place, parts):
    rows, lanes = parts[0].shape
    chips = rows // HEAD_DIM
    return pl.pallas_call(
        functools.partial(sum_heads_kernel, chips),
        in_specs=[SMEM] + [VMEM] * len(parts),
        out_specs=[VMEM] * chips,
        out_shape=[jax.ShapeDtypeStruct((HEAD_DIM, lanes), F32 if d == 0 else BF) for d in range(chips)],
        scratch_shapes=[pltpu.VMEM((rows, lanes), F32)],
        name="sum_heads",
        **params(16),
    )(place, *parts)


def sum_columns_kernel(place, *rest):
    parts, (keep, send, wide) = rest[:-3], rest[-3:]
    wide[...] = added(parts)
    lanes = keep.shape[1]
    keep[...] = wide[:, aligned(place[5], lanes)]
    send[...] = wide[:, aligned(1 - place[5], lanes)].astype(BF)


def sum_columns(place, parts):
    rows, lanes = parts[0].shape
    return pl.pallas_call(
        sum_columns_kernel,
        in_specs=[SMEM] + [VMEM] * len(parts),
        out_specs=[VMEM] * 2,
        out_shape=[jax.ShapeDtypeStruct((rows, lanes // 2), F32), jax.ShapeDtypeStruct((rows, lanes // 2), BF)],
        scratch_shapes=[pltpu.VMEM((rows, lanes), F32)],
        name="sum_columns",
        **params(16),
    )(place, *parts)


def shifted(parts, axis, sign):
    size = len(parts)
    return [parts[0]] + [
        lax.ppermute(parts[d], axis, [(i, (i + sign * d) % size) for i in range(size)]) for d in range(1, size)
    ]


def shards(tokens, covisible, w_query, w_key, w_value, w_out, cotangent):
    chips = lax.axis_size("fx")
    assert chips == 4
    swap = [(0, 1), (1, 0)]
    x, z, core, y, low = (lax.axis_index(name) for name in ("fx", "fz", "fc", "sy", "sl"))
    place = jnp.stack([x, z, core, z * 2 + core, y, low]).astype(jnp.int32)

    def across(part, axis):
        return lax.ppermute(part, axis, swap)

    weights = fetch(place, (w_key, w_value, w_query, w_out), chips)
    far_tokens, far_cotangent = across(tokens, "fz"), across(cotangent, "fz")
    peer_tokens, peer_cotangent = across(tokens, "fc"), across(cotangent, "fc")
    near = shifted(project(place, (tokens, peer_tokens), (cotangent, peer_cotangent), weights, chips), "fx", 1)
    near[1], far_tokens, far_cotangent = lax.optimization_barrier((near[1], far_tokens, far_cotangent))
    far_peer_tokens, far_peer_cotangent = across(far_tokens, "fc"), across(far_cotangent, "fc")
    far = shifted(
        project(place, (far_tokens, far_peer_tokens), (far_cotangent, far_peer_cotangent), weights, chips), "fx", 1
    )

    terms = shifted(attend(place, covisible, near + far, chips), "fx", -1)

    cotangents = (cotangent, peer_cotangent, far_cotangent, far_peer_cotangent)
    cuts = out_terms(place, terms, cotangents, lax.axis_size("sy"))
    terms, cuts = lax.optimization_barrier((terms, cuts))
    cuts = shifted(cuts, "sy", 1)
    own, far_own, away = finish(place, terms, weights)
    sent, cuts = lax.optimization_barrier((across(away, "fc"), cuts))
    rows, width = tokens.shape
    far_sum = (far_own + sent[rows:].astype(F32)).astype(BF)
    cuts, _ = lax.optimization_barrier((cuts, far_sum))
    far_sum = across(far_sum, "fz")
    tiles = shifted(sum_heads(place, cuts), "fx", 1)
    tile, other = sum_columns(place, tiles)
    grad_out_weight = tile + across(other, "sl").astype(F32)
    grad_tokens, result = (
        own[:, part] + sent[:rows, part].astype(F32) + far_sum[:, part].astype(F32)
        for part in (slice(0, width), slice(width, 2 * width))
    )
    return (result.astype(BF), grad_tokens, grad_out_weight)


def solution(mesh):
    names = ("sy", "sl", "fx", "fz", "fc")
    split = jax.sharding.Mesh(mesh.devices.reshape(-1, 2, 4, 2, 2), names)
    rows = P(names, None)
    in_specs = (rows, P(names[:2], None, None), P(), P(), P(), P(), rows)
    out_specs = (rows, rows, P(names[2:], names[:2]))
    return jax.shard_map(shards, mesh=split, in_specs=in_specs, out_specs=out_specs, check_vma=False)
```

```python
import functools
import math

import jax
import jax.numpy as jnp
from jax import lax
from jax.experimental import pallas as pl
from jax.experimental.pallas import tpu as pltpu
from jax.sharding import PartitionSpec as P

HEAD_DIM = 64
BF = jnp.bfloat16
F32 = jnp.float32
HIDDEN = -1e30
NT = (((1,), (1,)), ((), ()))
VMEM = pl.BlockSpec(memory_space=pltpu.VMEM)
SMEM = pl.BlockSpec(memory_space=pltpu.SMEM)
ANY = pl.BlockSpec(memory_space=pl.ANY)
LOG2E = 1.0 / math.log(2.0)
SCALE = HEAD_DIM**-0.5


def dot(a, b):
    return jnp.dot(a, b, preferred_element_type=F32)


def dot_nt(a, b):
    return lax.dot_general(a, b, NT, preferred_element_type=F32)


def params(limit):
    return dict(
        compiler_params=pltpu.CompilerParams(vmem_limit_bytes=limit * 2**20),
        cost_estimate=pl.CostEstimate(flops=1, bytes_accessed=1, transcendentals=0),
    )


def start_all(pairs, arrived):
    copies = [pltpu.make_async_copy(src, dst, arrived.at[i]) for i, (src, dst) in enumerate(pairs)]
    for copy in copies:
        copy.start()
    return copies


def aligned(index, size):
    return pl.ds(pl.multiple_of(index * size, size), size)


def in_core_order(place, rows_ref, start, own, peer):
    rows = own.shape[0]
    core = place[2]
    rows_ref[pl.ds(pl.multiple_of(start + core * rows, rows), rows), :] = own[...]
    rows_ref[pl.ds(pl.multiple_of(start + (1 - core) * rows, rows), rows), :] = peer[...]


def fetch_kernel(place, wk, wv, wq, wo, columns, rows, pairs, arrived):
    z, core, block = place[1], place[2], place[3]
    chips = pairs.shape[1]
    wide = 2 * HEAD_DIM
    moves = [
        (w.at[:, pl.ds(pl.multiple_of(a * 2 * wide + z * wide, wide), wide)], pairs.at[slot, a])
        for slot, w in enumerate((wk, wv, wq))
        for a in range(chips)
    ]
    for a in range(chips):
        from_rows = aligned(chips * a + block, HEAD_DIM)
        moves.append((wo.at[from_rows, :], rows.at[a * HEAD_DIM : (a + 1) * HEAD_DIM, :]))
    copies = start_all(moves, arrived)

    def keep(slot, lanes):
        for a in range(0, chips, 2):
            both = jnp.concatenate([pairs[slot, a, :, lanes], pairs[slot, a + 1, :, lanes]], axis=1)
            columns[slot, :, a * HEAD_DIM : (a + 2) * HEAD_DIM] = both

    for slot in range(3):
        for a in range(chips):
            copies[slot * chips + a].wait()
        pl.when(core == 0)(functools.partial(keep, slot, slice(0, HEAD_DIM)))
        pl.when(core == 1)(functools.partial(keep, slot, slice(HEAD_DIM, wide)))
    for copy in copies[3 * chips :]:
        copy.wait()


def fetch(place, weights, chips):
    width = weights[0].shape[0]
    block = chips * HEAD_DIM
    return pl.pallas_call(
        fetch_kernel,
        in_specs=[SMEM] + [ANY] * 4,
        out_specs=[VMEM] * 2,
        out_shape=[jax.ShapeDtypeStruct((3, width, block), BF), jax.ShapeDtypeStruct((block, width), BF)],
        scratch_shapes=[
            pltpu.VMEM((3, chips, width, 2 * HEAD_DIM), BF),
            pltpu.SemaphoreType.DMA((4 * chips,)),
        ],
        name="fetch",
        **params(48),
    )(place, *weights)


def project_kernel(place, own, peer, cot, peer_cot, held, held_out, *rest):
    outs, (tok, grads, turned) = rest[:-3], rest[-3:]
    in_core_order(place, tok, 0, own, peer)
    in_core_order(place, grads, 0, cot, peer_cot)
    for slot in range(3):
        part = dot(tok[...], held[slot])
        if slot == 2:
            part = part * (SCALE * LOG2E)
        turned[slot] = part.astype(BF).T
    turned[3] = dot_nt(held_out[...], grads[...]).astype(BF)
    for d, out in enumerate(outs):
        head = lax.rem(place[0] + d, len(outs))
        for slot in range(4):
            out[slot * HEAD_DIM : (slot + 1) * HEAD_DIM, :] = turned[slot, aligned(head, HEAD_DIM), :]


def project(place, tokens, cotangents, weights, chips):
    rows, width = tokens[0].shape
    block = chips * HEAD_DIM
    return pl.pallas_call(
        project_kernel,
        in_specs=[SMEM] + [VMEM] * 6,
        out_specs=[VMEM] * chips,
        out_shape=[jax.ShapeDtypeStruct((4 * HEAD_DIM, 2 * rows), BF)] * chips,
        scratch_shapes=[
            pltpu.VMEM((2 * rows, width), BF),
            pltpu.VMEM((2 * rows, width), BF),
            pltpu.VMEM((4, block, 2 * rows), BF),
        ],
        name="project",
        **params(16),
    )(place, *tokens, *cotangents, *weights)


def frame_at(place, chips, slot, core):
    plane, d = slot // chips, slot % chips
    x = lax.rem(place[0] + chips - d, chips)
    z = lax.rem(place[1] + plane, 2)
    return x * 4 + z * 2 + core


def attend_kernel(chips, step, chunk, place, cov, *rest):
    slots = 2 * chips
    parts, outs, rest = rest[:slots], rest[slots : slots + chips], rest[slots + chips :]
    packed, keys, even, odd, raw_even, raw_odd, att, grad_query, total = rest
    rows = slots * step
    frame_rows = step // 2
    frames = 2 * slots
    lane = lax.broadcasted_iota(jnp.int32, (step, 128), 1)
    half = lax.broadcasted_iota(jnp.int32, (step, 128), 0) // frame_rows
    ones = (lane >= frames) & (lane < frames + 3)
    for slot, part in enumerate(parts):
        at = slot * step
        packed[:, at : at + step] = part[...]
        keys[at : at + step, 0:128] = part[0:128, :].T
        keys[at : at + step, 128:256] = jnp.where((lane == half + 2 * slot) | ones, 1.0, 0.0).astype(BF)
    total[...] = jnp.zeros_like(total)
    chunks = range(0, rows, chunk)
    bias_row = lax.broadcasted_iota(jnp.int32, (frames, frame_rows), 0)
    delta_row = lax.broadcasted_iota(jnp.int32, (16, step), 0)
    rest_rows = jnp.zeros((128 - frames, step), BF)
    last_rows = jnp.zeros((112 - frames, step), BF)
    frame_zeros = jnp.zeros((frames, step), BF)
    sum_rows = jnp.ones((16, chunk), BF)
    zero = jnp.zeros((HEAD_DIM, step), F32)
    none = jnp.zeros((HEAD_DIM, step), BF)

    def columns(ref, first, i):
        return ref[first : first + HEAD_DIM, pl.ds(pl.multiple_of(i * step, step), step)]

    def score_side(i):
        biases = []
        for core in range(2):
            query_frame = frame_at(place, chips, i, core)
            bias = jnp.zeros((frames, frame_rows), F32)
            for key in range(frames):
                key_frame = frame_at(place, chips, key // 2, key % 2)
                seen = jnp.logical_or(cov[0, query_frame, key_frame] == 1, query_frame == key_frame)
                bias = jnp.where(bias_row == key, jnp.where(seen, 0.0, HIDDEN), bias)
            biases.append(bias)
        bias = jnp.concatenate(biases, axis=1).astype(BF)
        return jnp.concatenate([columns(packed, 128, i), none, bias, rest_rows], axis=0)

    def grad_sides(i, inverse, delta):
        grad = columns(packed, 192, i)
        high = delta.astype(BF).astype(F32)
        middle = (delta - high).astype(BF).astype(F32)
        low = delta - high - middle
        deltas = jnp.where(
            delta_row == 0, -high, jnp.where(delta_row == 1, -middle, jnp.where(delta_row == 2, -low, 0.0))
        ).astype(BF)
        query = columns(packed, 128, i).astype(F32) * (inverse * (1.0 / LOG2E))
        back = jnp.concatenate(
            [
                jnp.concatenate([zero, grad.astype(F32) * inverse], axis=0).astype(BF).T,
                jnp.concatenate([query, zero], axis=0).astype(BF).T,
            ],
            axis=0,
        )
        return jnp.concatenate([none, grad, frame_zeros, deltas, last_rows], axis=0), back

    def together(score=None, weigh=None, grad=None):
        if score:
            at_score, logits_to = score
            score_right = score_side(at_score)
            top = jnp.full((8, step), HIDDEN, F32)
        if weigh:
            at_weigh, logits_from, weigh_top, raw_to = weigh
            summed = jnp.zeros((HEAD_DIM + 16, step), F32)
        if grad:
            at_grad, raw_from, inverse, delta = grad
            grad_right, back = grad_sides(at_grad, inverse, delta)
            query_sum = zero
        for c in chunks:
            here = slice(c, c + chunk)
            if score:
                part = dot(keys[here, :], score_right)
                logits_to[here, :] = part
                top = jnp.maximum(top, jnp.max(part.reshape(chunk // 8, 8, step), axis=0))
            if weigh:
                raw = jnp.exp2(logits_from[here, :] - weigh_top).astype(BF)
                raw_to[here, :] = raw
                summed = summed + dot(jnp.concatenate([packed[HEAD_DIM:128, here], sum_rows], axis=0), raw)
            if grad:
                raw = raw_from[here, :]
                change = raw * dot(keys[here, :], grad_right).astype(BF)
                query_sum = query_sum + dot(packed[0:HEAD_DIM, here], change)
                total[here, :] += dot(jnp.concatenate([raw, change], axis=1), back)
        if grad:
            at = pl.ds(pl.multiple_of(at_grad * step, step), step)
            grad_query[:, at] = (query_sum * (inverse * SCALE)).astype(BF)
        got = ()
        if score:
            got += (jnp.max(top, axis=0, keepdims=True),)
        if weigh:
            inverse = 1.0 / summed[HEAD_DIM : HEAD_DIM + 1, :]
            attended = summed[0:HEAD_DIM, :] * inverse
            att[:, pl.ds(pl.multiple_of(at_weigh * step, step), step)] = attended.astype(BF)
            delta = jnp.sum(columns(packed, 192, at_weigh).astype(F32) * attended, axis=0, keepdims=True)
            got += (inverse, delta)
        return got

    (top,) = together(score=(0, even))
    carry = together(score=(1, odd), weigh=(0, even, top, raw_even))

    def body(j, carry):
        i = 2 * j + 1
        top, inverse, delta = carry
        top, inverse, delta = together((i + 1, even), (i, odd, top, raw_odd), (i - 1, raw_even, inverse, delta))
        return together((i + 2, odd), (i + 1, even, top, raw_even), (i, raw_odd, inverse, delta))

    top, inverse, delta = lax.fori_loop(0, slots // 2 - 1, body, carry)
    inverse, delta = together(
        weigh=(slots - 1, odd, top, raw_odd), grad=(slots - 2, raw_even, inverse, delta)
    )
    together(grad=(slots - 1, raw_odd, inverse, delta))
    for slot in range(slots):
        here = slice(slot * step, (slot + 1) * step)
        there = slice(slot // chips * step, (slot // chips + 1) * step)
        out = outs[slot % chips]
        out[0:HEAD_DIM, there] = grad_query[:, here]
        out[HEAD_DIM : 3 * HEAD_DIM, there] = total[here, :].astype(BF).T
        out[3 * HEAD_DIM : 4 * HEAD_DIM, there] = att[:, here]


def attend(place, pairs, parts, chips):
    step = parts[0].shape[1]
    slots = 2 * chips
    rows = slots * step
    return pl.pallas_call(
        functools.partial(attend_kernel, chips, step, 1024),
        in_specs=[SMEM, SMEM] + [VMEM] * slots,
        out_specs=[VMEM] * chips,
        out_shape=[jax.ShapeDtypeStruct((4 * HEAD_DIM, 2 * step), BF)] * chips,
        scratch_shapes=[
            pltpu.VMEM((4 * HEAD_DIM, rows), BF),
            pltpu.VMEM((rows, 256), BF),
            pltpu.VMEM((rows, step), F32),
            pltpu.VMEM((rows, step), F32),
            pltpu.VMEM((rows, step), BF),
            pltpu.VMEM((rows, step), BF),
            pltpu.VMEM((HEAD_DIM, rows), BF),
            pltpu.VMEM((HEAD_DIM, rows), BF),
            pltpu.VMEM((rows, 128), F32),
        ],
        name="attend",
        **params(40),
    )(place, pairs, *parts)


def finish_kernel(place, held, held_out, *rest):
    parts, (near, far, send, turned, wide) = rest[:-5], rest[-5:]
    chips = len(parts)
    rows, width = near.shape[0], held.shape[1]
    core = place[2]
    for d, part in enumerate(parts):
        head = lax.rem(place[0] + d, chips)
        for slot in range(4):
            turned[slot, aligned(head, HEAD_DIM), :] = part[slot * HEAD_DIM : (slot + 1) * HEAD_DIM, :]
    terms = None
    for slot, weight in enumerate((2, 0, 1)):
        term = dot_nt(turned[slot].T, held[weight])
        terms = term if terms is None else terms + term
    wide[:, 0:width] = terms
    wide[:, width : 2 * width] = dot(turned[3].T, held_out[...])
    near[...] = wide[aligned(core, rows), :]
    far[...] = wide[aligned(2 + core, rows), :]
    send[0:rows, :] = wide[aligned(1 - core, rows), :].astype(BF)
    send[rows : 2 * rows, :] = wide[aligned(3 - core, rows), :].astype(BF)


def finish(place, parts, weights):
    chips = len(parts)
    rows, width = parts[0].shape[1] // 4, weights[0].shape[1]
    block = chips * HEAD_DIM
    keep = jax.ShapeDtypeStruct((rows, 2 * width), F32)
    return pl.pallas_call(
        finish_kernel,
        in_specs=[SMEM] + [VMEM] * (2 + chips),
        out_specs=[VMEM] * 3,
        out_shape=[keep, keep, jax.ShapeDtypeStruct((2 * rows, 2 * width), BF)],
        scratch_shapes=[pltpu.VMEM((4, block, 4 * rows), BF), pltpu.VMEM((4 * rows, 2 * width), F32)],
        name="finish",
        **params(24),
    )(place, *weights, *parts)


def out_terms_kernel(place, *rest):
    parts, cots, rest = rest[0:4], rest[4:8], rest[8:]
    outs, (turned, cot, wide) = rest[:-3], rest[-3:]
    rows = cots[0].shape[0]
    in_core_order(place, cot, 0, cots[0], cots[1])
    in_core_order(place, cot, 2 * rows, cots[2], cots[3])
    for d, part in enumerate(parts):
        turned[aligned(lax.rem(place[0] + d, len(parts)), HEAD_DIM), :] = part[3 * HEAD_DIM : 4 * HEAD_DIM, :]
    wide[...] = dot(turned[...], cot[...])
    for d, out in enumerate(outs):
        out[...] = wide[:, aligned(lax.rem(place[4] + d, len(outs)), out.shape[1])].astype(BF)


def out_terms(place, parts, cotangents, cuts):
    chips = len(parts)
    rows, width = cotangents[0].shape
    block = chips * HEAD_DIM
    return pl.pallas_call(
        out_terms_kernel,
        in_specs=[SMEM] + [VMEM] * (chips + 4),
        out_specs=[VMEM] * cuts,
        out_shape=[jax.ShapeDtypeStruct((block, width // cuts), BF)] * cuts,
        scratch_shapes=[
            pltpu.VMEM((block, 4 * rows), BF),
            pltpu.VMEM((4 * rows, width), BF),
            pltpu.VMEM((block, width), F32),
        ],
        name="out_terms",
        **params(16),
    )(place, *parts, *cotangents)


def added(parts):
    total = parts[0][...].astype(F32)
    for part in parts[1:]:
        total = total + part[...].astype(F32)
    return total


def sum_heads_kernel(chips, place, *rest):
    parts, outs, wide = rest[: -1 - chips], rest[-1 - chips : -1], rest[-1]
    wide[...] = added(parts)
    for d, out in enumerate(outs):
        out[...] = wide[aligned(lax.rem(place[0] + d, chips), HEAD_DIM), :].astype(out.dtype)


def sum_heads(place, parts):
    rows, lanes = parts[0].shape
    chips = rows // HEAD_DIM
    return pl.pallas_call(
        functools.partial(sum_heads_kernel, chips),
        in_specs=[SMEM] + [VMEM] * len(parts),
        out_specs=[VMEM] * chips,
        out_shape=[jax.ShapeDtypeStruct((HEAD_DIM, lanes), F32 if d == 0 else BF) for d in range(chips)],
        scratch_shapes=[pltpu.VMEM((rows, lanes), F32)],
        name="sum_heads",
        **params(16),
    )(place, *parts)


def sum_columns_kernel(place, *rest):
    parts, (keep, send, wide) = rest[:-3], rest[-3:]
    wide[...] = added(parts)
    lanes = keep.shape[1]
    keep[...] = wide[:, aligned(place[5], lanes)]
    send[...] = wide[:, aligned(1 - place[5], lanes)].astype(BF)


def sum_columns(place, parts):
    rows, lanes = parts[0].shape
    return pl.pallas_call(
        sum_columns_kernel,
        in_specs=[SMEM] + [VMEM] * len(parts),
        out_specs=[VMEM] * 2,
        out_shape=[jax.ShapeDtypeStruct((rows, lanes // 2), F32), jax.ShapeDtypeStruct((rows, lanes // 2), BF)],
        scratch_shapes=[pltpu.VMEM((rows, lanes), F32)],
        name="sum_columns",
        **params(16),
    )(place, *parts)


def shifted(parts, axis, sign):
    size = len(parts)
    return [parts[0]] + [
        lax.ppermute(parts[d], axis, [(i, (i + sign * d) % size) for i in range(size)]) for d in range(1, size)
    ]


def shards(tokens, covisible, w_query, w_key, w_value, w_out, cotangent):
    chips = lax.axis_size("fx")
    assert chips == 4
    swap = [(0, 1), (1, 0)]
    x, z, core, y, low = (lax.axis_index(name) for name in ("fx", "fz", "fc", "sy", "sl"))
    place = jnp.stack([x, z, core, z * 2 + core, y, low]).astype(jnp.int32)

    def across(part, axis):
        return lax.ppermute(part, axis, swap)

    weights = fetch(place, (w_key, w_value, w_query, w_out), chips)
    far_tokens, far_cotangent = across(tokens, "fz"), across(cotangent, "fz")
    peer_tokens, peer_cotangent = across(tokens, "fc"), across(cotangent, "fc")
    near = shifted(project(place, (tokens, peer_tokens), (cotangent, peer_cotangent), weights, chips), "fx", 1)
    near[1], far_tokens, far_cotangent = lax.optimization_barrier((near[1], far_tokens, far_cotangent))
    far_peer_tokens, far_peer_cotangent = across(far_tokens, "fc"), across(far_cotangent, "fc")
    far = shifted(
        project(place, (far_tokens, far_peer_tokens), (far_cotangent, far_peer_cotangent), weights, chips), "fx", 1
    )

    terms = shifted(attend(place, covisible, near + far, chips), "fx", -1)

    cotangents = (cotangent, peer_cotangent, far_cotangent, far_peer_cotangent)
    cuts = out_terms(place, terms, cotangents, lax.axis_size("sy"))
    terms, cuts = lax.optimization_barrier((terms, cuts))
    cuts = shifted(cuts, "sy", 1)
    own, far_own, away = finish(place, terms, weights)
    sent, cuts[2] = lax.optimization_barrier((across(away, "fc"), cuts[2]))
    rows, width = tokens.shape
    far_sum = (far_own + sent[rows:].astype(F32)).astype(BF)
    cuts, _ = lax.optimization_barrier((cuts, far_sum))
    far_sum = across(far_sum, "fz")
    tiles = shifted(sum_heads(place, cuts), "fx", 1)
    tile, other = sum_columns(place, tiles)
    grad_out_weight = tile + across(other, "sl").astype(F32)
    grad_tokens, result = (
        own[:, part] + sent[:rows, part].astype(F32) + far_sum[:, part].astype(F32)
        for part in (slice(0, width), slice(width, 2 * width))
    )
    return (result.astype(BF), grad_tokens, grad_out_weight)


def solution(mesh):
    names = ("sy", "sl", "fx", "fz", "fc")
    split = jax.sharding.Mesh(mesh.devices.reshape(-1, 2, 4, 2, 2), names)
    rows = P(names, None)
    in_specs = (rows, P(names[:2], None, None), P(), P(), P(), P(), rows)
    out_specs = (rows, rows, P(names[2:], names[:2]))
    return jax.shard_map(shards, mesh=split, in_specs=in_specs, out_specs=out_specs, check_vma=False)
```
